512 devices in a mesh: groups: 64 (over z_hi, y, core), tensor: 8 (over x, z_lo).
Axes of the slice: x: 4, y: 8, z: 8 (z_hi: 4, z_lo: 2; z = z_hi * 2 + z_lo), core: 2. Of those that a mesh axis runs over, the one named last changes fastest.
Arguments:
- tokens_old: bfloat16 [256, 8192], P('groups', 'tensor'), may hold values from -32 to 32
- tokens_new: bfloat16 [256, 8192], P('groups', 'tensor'), may hold values from -32 to 32
- norm_gain: float32 [8192], P('tensor'), may hold values from 0.1 to 1.9
- gate_base: bfloat16 [8192, 28672], P('tensor', 'groups'), may hold values from -0.0625 to 0.0625
- up_base: bfloat16 [8192, 28672], P('tensor', 'groups'), may hold values from -0.0625 to 0.0625
- down_base: bfloat16 [28672, 8192], P('groups', 'tensor'), may hold values from -0.03125 to 0.03125
- gate_left: bfloat16 [8192, 64], P(('tensor', 'groups')), may hold values from -0.0625 to 0.0625
- gate_right: bfloat16 [64, 28672], P(None, 'groups'), may hold values from -0.75 to 0.75
- up_left: bfloat16 [8192, 64], P(('tensor', 'groups')), may hold values from -0.0625 to 0.0625
- up_right: bfloat16 [64, 28672], P(None, 'groups'), may hold values from -0.75 to 0.75
- down_left: bfloat16 [28672, 64], P('groups'), may hold values from -0.03125 to 0.03125
- down_right: bfloat16 [8192, 64], P(('tensor', 'groups')), may hold values from -0.75 to 0.75
Outputs:
- out_old: bfloat16 [256, 8192], P('groups', 'tensor')
- out_new: bfloat16 [256, 8192], P('groups', 'tensor')
The draws below stay inside these ranges and needn't reach their ends.
All inputs are finite; a program needn't handle non-finite values.
Results may differ from the reference program's by a relative error of at most 0.0082.
Values may be sent and summed in bfloat16 or wider, within the bound.
A program may use at most 64 MiB of HBM per device.

```python
import jax
import jax.numpy as jnp
from jax import lax

D = 8192
FF = 28672
R = 64
ALPHA = 32
ROWS = 256


def shape_field(noise_field, row_scale, column_key):
    column_pos = jnp.arange(D, dtype=jnp.float32) / D
    jitter = jax.random.uniform(column_key, (1, D), minval=-0.35, maxval=0.35)
    column_scale = 0.5 * jnp.exp(column_pos[None, :] * jnp.log(3.0) + jitter)
    return (noise_field * row_scale * column_scale).astype(jnp.bfloat16)


def draw_tokens_old(key, part):
    key = jax.random.fold_in(key, 11)
    subkeys = jax.random.split(key, 3)
    noise_field = jnp.clip(jax.random.normal(subkeys[0], (ROWS, D)), -4.0, 4.0)
    row_scale = jnp.exp(jax.random.uniform(subkeys[1], (ROWS, 1), minval=jnp.log(0.3), maxval=jnp.log(3.0)))
    return shape_field(noise_field, row_scale, subkeys[2])


def draw_tokens_new(key, part):
    key = jax.random.fold_in(key, 23)
    subkeys = jax.random.split(key, 3)
    noise_field = jnp.clip(jax.random.normal(subkeys[0], (ROWS, D)), -4.0, 4.0)
    row_scale = jnp.exp(jax.random.uniform(subkeys[1], (ROWS, 1), minval=jnp.log(0.3), maxval=jnp.log(3.0)))
    return shape_field(noise_field, row_scale, subkeys[2])


def block_scale(own_key, shape, cuts, least, largest):
    def one(dim, shards_of):
        heights = jax.random.uniform(jax.random.fold_in(jax.random.fold_in(own_key, 6), dim), (shards_of,), jnp.float32, least / len(cuts), largest / len(cuts))
        return jnp.repeat(jnp.exp(heights), shape[dim] // shards_of).reshape((-1,) + (1,) * (len(shape) - dim - 1))

    gain = one(*cuts[0])
    for cut in cuts[1:]:
        gain = gain * one(*cut)
    return gain


def noise(own_key, dims, scale, most, pieces=(), held_as=jnp.bfloat16):
    factor_of = block_scale(own_key, dims, pieces, -0.22, 0.18) if pieces else 1.0
    result = jax.random.normal(own_key, dims, jnp.float32) * scale * factor_of
    return jnp.minimum(jnp.maximum(result, -most), most).astype(held_as)


def setup_inputs(seed: int = 0) -> dict:
    keys = jax.random.split(jax.random.key(seed), 13)
    tokens_old = draw_tokens_old(jax.random.fold_in(keys[12], 71), 0)
    tokens_new = draw_tokens_new(jax.random.fold_in(keys[12], 71), 0)
    norm_gain = jnp.clip(1.0 + 0.18 * jax.random.normal(keys[2], (D,), jnp.float32), 0.1, 1.9)
    gate_base = noise(keys[3], (D, FF), D ** -0.5, 0.0625, ((0, 8), (1, 64)))
    up_base = noise(keys[4], (D, FF), D ** -0.5, 0.0625, ((0, 8), (1, 64)))
    down_base = noise(keys[5], (FF, D), FF ** -0.5, 0.03125, ((0, 64), (1, 8)))
    gate_left = noise(keys[6], (D, R), D ** -0.5, 0.0625, ((0, 512),))
    gate_right = noise(keys[7], (R, FF), R ** -0.5, 0.75, ((1, 64),))
    up_left = noise(keys[8], (D, R), D ** -0.5, 0.0625, ((0, 512),))
    up_right = noise(keys[9], (R, FF), R ** -0.5, 0.75, ((1, 64),))
    down_left = noise(keys[10], (FF, R), FF ** -0.5, 0.03125, ((0, 64),))
    down_right = noise(keys[11], (D, R), R ** -0.5, 0.75, ((0, 512),))
    return {"tokens_old": tokens_old, "tokens_new": tokens_new, "norm_gain": norm_gain, "gate_base": gate_base, "up_base": up_base, "down_base": down_base, "gate_left": gate_left, "gate_right": gate_right, "up_left": up_left, "up_right": up_right, "down_left": down_left, "down_right": down_right}


def merge_weight(base_shard, left_factor, right_factor):
    product = jnp.dot(left_factor, right_factor, preferred_element_type=jnp.float32)
    return (base_shard.astype(jnp.float32) + ALPHA / R * product).astype(jnp.bfloat16)

def decode(tokens, norm_gain, gate_weight, up_weight, down_weight):
    values = tokens.astype(jnp.float32)
    inverse = lax.rsqrt(lax.optimization_barrier(jnp.sum(values * values, axis=1, keepdims=True)) / D + 1e-05)
    scaled = (values * norm_gain).astype(jnp.bfloat16)
    gate_sum = jnp.dot(scaled, gate_weight, preferred_element_type=jnp.float32) * inverse
    up_sum = jnp.dot(scaled, up_weight, preferred_element_type=jnp.float32) * inverse
    hidden = (jax.nn.silu(gate_sum) * up_sum).astype(jnp.bfloat16)
    return jnp.dot(hidden, down_weight, preferred_element_type=jnp.float32).astype(jnp.bfloat16)

def reference(tokens_old, tokens_new, norm_gain, gate_base, up_base, down_base, gate_left, gate_right, up_left, up_right, down_left, down_right):
    out_old = decode(tokens_old, norm_gain, gate_base, up_base, down_base)
    gate_merged = merge_weight(gate_base, gate_left, gate_right)
    up_merged = merge_weight(up_base, up_left, up_right)
    down_merged = merge_weight(down_base, down_left, down_right.T)
    out_new = decode(tokens_new, norm_gain, gate_merged, up_merged, down_merged)
    return (out_old, out_new)
```

```python
import functools

import jax
import jax.numpy as jnp
from jax import lax
from jax.experimental import pallas as pl
from jax.experimental.pallas import tpu as pltpu
from jax.sharding import PartitionSpec as P

MESH = pl.DeviceIdType.MESH
F32, BF16 = jnp.float32, jnp.bfloat16
D = 8192
R = 64
ALPHA = 32
NZ, NY, NT = 4, 8, 8
DL, FL = 1024, 448
ROWS, OWN = 256, 4
HALF = ROWS // 2
BLOCK = ROWS // NT
LANES = 128
CHUNKS = DL // LANES
Z_ORDER = (2, 1, 3)
Y_ORDER = (4, 3, 5, 2, 6, 1, 7)


def block_target(b):
    x = b % 4
    return x * 2 + (b // 4 + x) % 2


def fold(values):
    return [values[:, j * LANES : (j + 1) * LANES] for j in range(CHUNKS)]


def kernel(
    old_ref, new_ref, gain_ref, gl_ref, ul_ref, dr_ref, gr_ref, ur_ref, dl_ref, gate_hbm, up_hbm, down_hbm,
    out_old_ref, out_new_ref,
    gate_v, up_v, down_v, w_old, w_new, down_new, rcomb,
    s1_old, s1_new, fac, x_old, x_new,
    p_old, p_new, t_old, t_new, h_old, h_new,
    d_own, d_sib_old, d_sib_new, e_old, e_new, cs_old, cs_new, r1_old, r1_new, c2_old, c2_new, r2_old, r2_new, inv_new,
    local_sem, ss, rs,
):
    g, t = lax.axis_index("groups"), lax.axis_index("tensor")
    zh, y, c = g // 16, (g // 2) % 8, g % 2
    pos = (t // 2) + 4 * ((t % 2 + t // 2) % 2)
    sibling = (zh * 16 + y * 2 + (1 - c), t)

    def z_peer(k):
        return (((zh + k) % NZ) * 16 + y * 2 + c, t)

    def y_peer(k):
        return (zh * 16 + ((y + k) % NY) * 2 + c, t)

    counter = [0]
    pending = {0: [], 1: [], None: []}

    def sems(n):
        counter[0] += n
        return counter[0] - n

    def remote(src, dst, s, r, dev):
        return pltpu.make_async_remote_copy(
            src_ref=src, dst_ref=dst, send_sem=ss.at[s], recv_sem=rs.at[r], device_id=dev, device_id_type=MESH
        )

    loads = [
        pltpu.make_async_copy(gate_hbm, gate_v, local_sem.at[0]),
        pltpu.make_async_copy(up_hbm, up_v, local_sem.at[1]),
        pltpu.make_async_copy(down_hbm, down_v, local_sem.at[2]),
    ]
    for load in loads:
        load.start()

    barrier = pltpu.get_barrier_semaphore()
    greet = [sibling] + [z_peer(k) for k in Z_ORDER] + [y_peer(k) for k in Y_ORDER]
    greet += [(g, (t + k) % NT) for k in range(1, NT)]
    for dev in greet:
        pl.semaphore_signal(barrier, inc=1, device_id=dev, device_id_type=MESH)

    lane = lax.broadcasted_iota(jnp.int32, (OWN, LANES), 1)
    sums = jnp.zeros((OWN, LANES), F32)
    gain = gain_ref[...]
    folded = []
    for i, ref in enumerate((old_ref, new_ref)):
        values = ref[...].astype(F32)
        square = jnp.sum(values * values, axis=1, keepdims=True)
        high = square.astype(BF16).astype(F32)
        sums = jnp.where(lane == 2 * i, high, sums)
        sums = jnp.where(lane == 2 * i + 1, square - high, sums)
        folded.append(fold(values * gain))
    zeros = jnp.zeros((48 - CHUNKS * OWN - OWN, LANES), F32)
    s1_old[0] = jnp.concatenate(folded[0] + [sums, zeros], axis=0).astype(BF16)
    s1_new[0] = jnp.concatenate(folded[1], axis=0).astype(BF16)
    left = jnp.concatenate([gl_ref[...], ul_ref[...]], axis=1)
    right = jnp.concatenate([dr_ref[...], jnp.zeros((16, LANES - R), BF16)], axis=1)
    fac[c, y, zh] = jnp.concatenate([left, right], axis=0)

    pl.semaphore_wait(barrier, len(greet))

    class Plane:
        def __init__(self, core):
            self.core = core
            first = (NZ, Z_ORDER, z_peer)
            second = (NY, Y_ORDER, y_peer)
            if core == 1:
                first, second = second, first
            self.n1, self.order1, self.peer1 = first
            self.n2, self.order2, self.peer2 = second
            self.rows = OWN * self.n1

        def block(self, k):
            return pl.ds(k * self.rows, self.rows)

        def record(self, copies):
            pending[self.core] += copies
            return copies

    planes = (Plane(0), Plane(1))
    base = {}
    for name in ("a1o", "a1n", "a1f", "a2o", "a2n", "a2f", "fo", "fn", "c1o", "c1n", "c2o", "c2n", "to", "tn", "ho", "hn"):
        base[name] = sems(8)
    for name in ("ff", "eo", "en"):
        base[name] = sems(1)

    def stage1(pln, name, src, dst_of):
        return [remote(src, dst_of(k), base[name] + k, base[name] + k, pln.peer1(k)) for k in pln.order1]

    def a1_copies(pln):
        return (
            [remote(s1_old.at[0], s1_old.at[k], base["a1o"] + k, base["a1o"] + k, pln.peer1(k)) for k in pln.order1],
            [remote(s1_new.at[0], s1_new.at[k], base["a1n"] + k, base["a1n"] + k, pln.peer1(k)) for k in pln.order1],
            [
                remote(fac.at[c, y, zh], fac.at[c, y, zh], base["a1f"] + k, base["a1f"] + k, pln.peer1(k))
                for k in pln.order1
            ],
        )

    def a2_copies(pln, name, x_ref):
        return [
            remote(x_ref.at[0, pln.block(0)], x_ref.at[0, pln.block(k)], base[name] + k, base[name] + k, pln.peer2(k))
            for k in pln.order2
        ]

    def a2_factor_copies(pln):
        part = fac.at[c, y] if pln.core == 0 else fac.at[c, :, zh]
        return [remote(part, part, base["a2f"] + k, base["a2f"] + k, pln.peer2(k)) for k in pln.order2]

    def forward(pln, name, x_ref, k):
        return remote(x_ref.at[0, pln.block(k)], x_ref.at[1, pln.block(k)], base[name] + k, base[name], sibling)

    def assemble(pln, s1, x_ref, chunks):
        parts = [s1[k].astype(F32) for k in range(pln.n1)]
        for j in range(chunks):
            tile = jnp.concatenate([part[OWN * j : OWN * (j + 1)] for part in parts], axis=0)
            x_ref[0, 0 : pln.rows, j * LANES : (j + 1) * LANES] = tile.astype(BF16)

    def per_core(fn):
        for pln in planes:
            pl.when(c == pln.core)(functools.partial(fn, pln))

    def gather_first(pln):
        olds, news, facs = a1_copies(pln)
        for copy in olds + news + facs:
            copy.start()
        for copy in olds:
            copy.wait_recv()
        assemble(pln, s1_old, x_old, CHUNKS + 1)
        for copy in a2_copies(pln, "a2o", x_old):
            copy.start()
        forward(pln, "fo", x_old, 0).start()
        for copy in news:
            copy.wait_recv()
        assemble(pln, s1_new, x_new, CHUNKS)
        for copy in a2_copies(pln, "a2n", x_new):
            copy.start()
        forward(pln, "fn", x_new, 0).start()
        for copy in facs:
            copy.wait_recv()
        for copy in a2_factor_copies(pln):
            copy.start()

    per_core(gather_first)

    loads[0].wait()
    loads[1].wait()

    def join(i, carry):
        part = pl.ds(i * 128, 128)
        w_old[part, :] = jnp.concatenate([gate_v[part, :], up_v[part, :]], axis=1)
        return carry

    lax.fori_loop(0, DL // 128, join, 0)
    none = jnp.zeros((R, FL), BF16)
    rcomb[0:R, :] = jnp.concatenate([gr_ref[...], none], axis=1)
    rcomb[R : 2 * R, :] = jnp.concatenate([none, ur_ref[...]], axis=1)

    def gather_second(pln, name, forward_name, x_ref):
        copies = a2_copies(pln, name, x_ref)
        for k, copy in reversed(list(zip(pln.order2, copies))):
            copy.wait_recv()
            forward(pln, forward_name, x_ref, k).start()

    def wait_sibling_half(name, x_ref):
        remote(x_ref.at[0], x_ref.at[1], base[name], base[name], sibling).wait_recv()

    def reduce_copy(name, p_ref, t_ref, b):
        return remote(p_ref.at[b], t_ref.at[pos], base[name] + b, base[name] + pos, (g, block_target(b)))

    def project(half, x_ref, w_ref, p_ref, t_ref, name, with_sums):
        product = jnp.dot(x_ref[half, :, 0:DL], w_ref[...], preferred_element_type=F32)
        p_ref[4 * half : 4 * half + 4, :, 0 : 2 * FL] = product.astype(BF16).reshape(4, BLOCK, 2 * FL)
        if with_sums:
            p_ref[4 * half : 4 * half + 4, :, 2 * FL :] = x_ref[half, :, DL:].reshape(4, BLOCK, LANES)
        for b in range(4 * half, 4 * half + 4):
            pl.when(b != pos)(lambda b=b: reduce_copy(name, p_ref, t_ref, b).start())

    def reduced(p_ref, t_ref, name):
        t_ref[pos] = p_ref[pos]
        for b in range(NT):
            def wait(b=b):
                remote(p_ref.at[b], t_ref.at[b], base[name] + b, base[name] + b, (g, block_target(b))).wait_recv()
            pl.when(b != pos)(wait)
        total = t_ref[0].astype(F32)
        for b in range(1, NT):
            total += t_ref[b].astype(F32)
        return total

    def hidden_copies(name, h_ref):
        copies = []
        for k in (6, 2, 5, 3, 7, 1, 4):
            b = (pos + k) % NT
            copies.append(remote(h_ref.at[pos], h_ref.at[pos], base[name] + b, base[name] + pos, (g, block_target(b))))
        return copies

    def activate(total, inverse, name, h_ref):
        gate = total[:, 0:FL] * inverse
        up = total[:, FL : 2 * FL] * inverse
        h_ref[pos] = (gate / (1.0 + jnp.exp(-gate)) * up).astype(BF16)
        for copy in hidden_copies(name, h_ref):
            copy.start()

    def wait_hidden(name, h_ref, half):
        for b in range(4 * half, 4 * half + 4):
            def wait(b=b):
                remote(h_ref.at[b], h_ref.at[b], base[name] + b, base[name] + b, (g, block_target(b))).wait_recv()
            pl.when(b != pos)(wait)

    def down_project(h_name, h_ref, down_ref, d_sib, e_ref, e_name, cs_ref):
        wait_hidden(h_name, h_ref, 1)
        d_sib[...] = jnp.dot(
            h_ref[4:8].reshape(HALF, FL), down_ref[...], preferred_element_type=F32
        ).astype(BF16)
        exchange = remote(d_sib, e_ref, base[e_name], base[e_name], sibling)
        exchange.start()
        wait_hidden(h_name, h_ref, 0)
        d_own[...] = jnp.dot(h_ref[0:4].reshape(HALF, FL), down_ref[...], preferred_element_type=F32)
        exchange.wait_recv()
        d_own[...] += e_ref[...].astype(F32)
        cs_ref[...] = d_own[...].astype(BF16)

    def c1_copies(pln, name, cs_ref, r1_ref):
        return [
            remote(cs_ref.at[pln.block(k)], r1_ref.at[pln.block(k)], base[name] + k, base[name] + k, pln.peer2(-k))
            for k in pln.order2
        ]

    def c2_copies(pln, name, c2_ref, r2_ref):
        return [
            remote(c2_ref.at[k], r2_ref.at[k], base[name] + k, base[name] + k, pln.peer1(-k)) for k in pln.order1
        ]

    def scatter_first(pln, name, cs_ref, r1_ref):
        for copy in c1_copies(pln, name, cs_ref, r1_ref):
            copy.start()

    def scatter_second(pln, name1, cs_ref, r1_ref, name2, c2_ref, r2_ref):
        for copy in c1_copies(pln, name1, cs_ref, r1_ref):
            copy.wait_recv()
        total = cs_ref[pln.block(0)].astype(F32)
        for k in range(1, pln.n2):
            total += r1_ref[pln.block(k)].astype(F32)
        for k in range(pln.n1):
            piece = jnp.concatenate(fold(total[OWN * k : OWN * (k + 1)]), axis=0)
            c2_ref[k] = piece.astype(BF16)
        for copy in c2_copies(pln, name2, c2_ref, r2_ref):
            copy.start()

    def scatter_last(pln, name2, c2_ref, r2_ref, out_ref):
        for copy in c2_copies(pln, name2, c2_ref, r2_ref):
            copy.wait_recv()
        total = c2_ref[0].astype(F32)
        for k in range(1, pln.n1):
            total += r2_ref[k].astype(F32)
        out_ref[...] = jnp.concatenate(
            [total[OWN * j : OWN * (j + 1)] for j in range(CHUNKS)], axis=1
        ).astype(BF16)

    per_core(lambda pln: gather_second(pln, "a2o", "fo", x_old))
    project(0, x_old, w_old, p_old, t_old, "to", True)
    wait_sibling_half("fo", x_old)
    project(1, x_old, w_old, p_old, t_old, "to", True)

    per_core(lambda pln: gather_second(pln, "a2n", "fn", x_new))

    def gather_factors(pln):
        for copy in a2_factor_copies(pln):
            copy.wait_recv()

    per_core(gather_factors)
    plane = fac.at[c]
    factor_exchange = remote(plane, plane, base["ff"], base["ff"], sibling)
    factor_exchange.start()
    factor_exchange.wait_recv()
    loads[2].wait()

    def merge_in(q):
        rows = pl.ds(q * 256, 256)
        left = jnp.concatenate([fac[i % 2, i // 2, q, 0:16, :] for i in range(16)], axis=0)
        product = jnp.dot(left, rcomb[...], preferred_element_type=F32)
        w_new[rows, :] = (w_old[rows, :].astype(F32) + ALPHA / R * product).astype(BF16)

    def merge_down(q):
        columns = pl.ds(q * 256, 256)
        right = jnp.concatenate([fac[i % 2, i // 2, q, 16:32, 0:R] for i in range(16)], axis=0)
        product = lax.dot_general(dl_ref[...], right, (((1,), (1,)), ((), ())), preferred_element_type=F32)
        down_new[:, columns] = (down_v[:, columns].astype(F32) + ALPHA / R * product).astype(BF16)

    for q in range(4):
        merge_in(q)
    project(0, x_new, w_new, p_new, t_new, "tn", False)
    wait_sibling_half("fn", x_new)
    project(1, x_new, w_new, p_new, t_new, "tn", False)

    total = reduced(p_old, t_old, "to")
    mean = total[:, 2 * FL :] * (1.0 / D)
    inverse_old = lax.rsqrt(mean[:, 0:1] + mean[:, 1:2] + 1e-05)
    inv_new[...] = jnp.broadcast_to(lax.rsqrt(mean[:, 2:3] + mean[:, 3:4] + 1e-05), (BLOCK, LANES))
    activate(total, inverse_old, "ho", h_old)
    for q in range(4):
        merge_down(q)
    down_project("ho", h_old, down_v, d_sib_old, e_old, "eo", cs_old)
    per_core(lambda pln: scatter_first(pln, "c1o", cs_old, r1_old))

    total = reduced(p_new, t_new, "tn")
    activate(total, inv_new[:, 0:1], "hn", h_new)
    per_core(lambda pln: scatter_second(pln, "c1o", cs_old, r1_old, "c2o", c2_old, r2_old))
    down_project("hn", h_new, down_new, d_sib_new, e_new, "en", cs_new)
    per_core(lambda pln: scatter_first(pln, "c1n", cs_new, r1_new))
    per_core(lambda pln: scatter_last(pln, "c2o", c2_old, r2_old, out_old_ref))
    per_core(lambda pln: scatter_second(pln, "c1n", cs_new, r1_new, "c2n", c2_new, r2_new))
    per_core(lambda pln: scatter_last(pln, "c2n", c2_new, r2_new, out_new_ref))

    def drain(pln):
        for group in a1_copies(pln):
            for copy in group:
                copy.wait_send()
        copies = a2_copies(pln, "a2o", x_old) + a2_copies(pln, "a2n", x_new) + a2_factor_copies(pln)
        copies += [forward(pln, "fo", x_old, k) for k in range(pln.n2)]
        copies += [forward(pln, "fn", x_new, k) for k in range(pln.n2)]
        copies += c1_copies(pln, "c1o", cs_old, r1_old) + c1_copies(pln, "c1n", cs_new, r1_new)
        copies += c2_copies(pln, "c2o", c2_old, r2_old) + c2_copies(pln, "c2n", c2_new, r2_new)
        for copy in copies:
            copy.wait_send()

    per_core(drain)
    factor_exchange.wait_send()
    remote(d_sib_old, e_old, base["eo"], base["eo"], sibling).wait_send()
    remote(d_sib_new, e_new, base["en"], base["en"], sibling).wait_send()
    for b in range(NT):
        def wait(b=b):
            reduce_copy("to", p_old, t_old, b).wait_send()
            reduce_copy("tn", p_new, t_new, b).wait_send()
        pl.when(b != pos)(wait)
    for copy in hidden_copies("ho", h_old) + hidden_copies("hn", h_new):
        copy.wait_send()


def per_device(old, new, gain, gate, up, down, gl, gr, ul, ur, dl, dr):
    vmem = pl.BlockSpec(memory_space=pltpu.VMEM)
    hbm = pl.BlockSpec(memory_space=pl.ANY)
    scratch = [
        ((DL, FL), BF16), ((DL, FL), BF16), ((FL, DL), BF16),
        ((DL, 2 * FL), BF16), ((DL, 2 * FL), BF16), ((FL, DL), BF16), ((2 * R, 2 * FL), BF16),
        ((8, 48, LANES), BF16), ((8, 32, LANES), BF16), ((2, NY, NZ, 32, LANES), BF16),
        ((2, HALF, DL + LANES), BF16), ((2, HALF, DL), BF16),
        ((NT, BLOCK, 2 * FL + LANES), BF16), ((NT, BLOCK, 2 * FL), BF16),
        ((NT, BLOCK, 2 * FL + LANES), BF16), ((NT, BLOCK, 2 * FL), BF16),
        ((NT, BLOCK, FL), BF16), ((NT, BLOCK, FL), BF16),
        ((HALF, DL), F32), ((HALF, DL), BF16), ((HALF, DL), BF16),
        ((HALF, DL), BF16), ((HALF, DL), BF16), ((HALF, DL), BF16), ((HALF, DL), BF16),
        ((HALF, DL), BF16), ((HALF, DL), BF16),
        ((8, 32, LANES), BF16), ((8, 32, LANES), BF16), ((8, 32, LANES), BF16), ((8, 32, LANES), BF16),
        ((BLOCK, LANES), F32),
    ]
    flops = 2 * (2 * ROWS * DL * FL * 3 + 3 * DL * FL * R)
    return pl.pallas_call(
        kernel,
        out_shape=[jax.ShapeDtypeStruct((OWN, DL), BF16)] * 2,
        in_specs=[vmem] * 9 + [hbm] * 3,
        out_specs=[vmem, vmem],
        scratch_shapes=[pltpu.VMEM(shape, dtype) for shape, dtype in scratch]
        + [pltpu.SemaphoreType.DMA((3,)), pltpu.SemaphoreType.DMA((132,)), pltpu.SemaphoreType.DMA((132,))],
        compiler_params=pltpu.CompilerParams(
            collective_id=0, has_side_effects=True, vmem_limit_bytes=48 * 1024 * 1024
        ),
        cost_estimate=pl.CostEstimate(flops=flops, bytes_accessed=6 * DL * FL, transcendentals=2 * BLOCK * FL),
    )(old, new, gain.reshape(1, DL), gl, ul, dr, gr, ur, dl, gate, up, down)


def solution(mesh):
    in_specs = (
        P("groups", "tensor"),
        P("groups", "tensor"),
        P("tensor"),
        P("tensor", "groups"),
        P("tensor", "groups"),
        P("groups", "tensor"),
        P(("tensor", "groups"), None),
        P(None, "groups"),
        P(("tensor", "groups"), None),
        P(None, "groups"),
        P("groups", None),
        P(("tensor", "groups"), None),
    )
    out_specs = (P("groups", "tensor"), P("groups", "tensor"))
    return jax.shard_map(per_device, mesh=mesh, in_specs=in_specs, out_specs=out_specs, check_vma=False)
```

```python
import functools

import jax
import jax.numpy as jnp
from jax import lax
from jax.experimental import pallas as pl
from jax.experimental.pallas import tpu as pltpu
from jax.sharding import PartitionSpec as P

MESH = pl.DeviceIdType.MESH
F32, BF16 = jnp.float32, jnp.bfloat16
D = 8192
R = 64
ALPHA = 32
NZ, NY, NT = 4, 8, 8
DL, FL = 1024, 448
ROWS, OWN = 256, 4
HALF = ROWS // 2
BLOCK = ROWS // NT
LANES = 128
CHUNKS = DL // LANES
Z_ORDER = (2, 1, 3)
Y_ORDER = (4, 3, 5, 2, 6, 1, 7)


def block_target(b):
    x = b % 4
    return x * 2 + (b // 4 + x) % 2


def fold(values):
    return [values[:, j * LANES : (j + 1) * LANES] for j in range(CHUNKS)]


def kernel(
    old_hbm, new_hbm, gain_hbm, gl_hbm, ul_hbm, dr_hbm, gr_hbm, ur_hbm, dl_hbm, gate_hbm, up_hbm, down_hbm,
    out_old_ref, out_new_ref,
    old_v, new_v, gain_v, gl_v, ul_v, dr_v, gr_v, ur_v, dl_v, w_in, down_v, down_new,
    s1_old, s1_new, left, right, x_old, x_new,
    p_old, p_new, p_low, t_old, t_new, t_low, h_old, h_new,
    d_own, d_sib_old, d_sib_new, e_old, e_new, cs_old, cs_new, r1_old, r1_new, c2_old, c2_new, r2_old, r2_new, inv_new,
    local_sem, ss, rs,
):
    g, t = lax.axis_index("groups"), lax.axis_index("tensor")
    zh, y, c = g // 16, (g // 2) % 8, g % 2
    pos = (t // 2) + 4 * ((t % 2 + t // 2) % 2)
    sibling = (zh * 16 + y * 2 + (1 - c), t)

    def z_peer(k):
        return (((zh + k) % NZ) * 16 + y * 2 + c, t)

    def y_peer(k):
        return (zh * 16 + ((y + k) % NY) * 2 + c, t)

    counter = [0]

    def sems(n):
        counter[0] += n
        return counter[0] - n

    def remote(src, dst, s, r, dev):
        return pltpu.make_async_remote_copy(
            src_ref=src, dst_ref=dst, send_sem=ss.at[s], recv_sem=rs.at[r], device_id=dev, device_id_type=MESH
        )

    barrier = pltpu.get_barrier_semaphore()
    greet = [sibling] + [z_peer(k) for k in Z_ORDER] + [y_peer(k) for k in Y_ORDER]
    greet += [(g, (t + k) % NT) for k in range(1, NT)]
    for dev in greet:
        pl.semaphore_signal(barrier, inc=1, device_id=dev, device_id_type=MESH)

    small = [
        pltpu.make_async_copy(src, dst, local_sem.at[6 + n])
        for n, (src, dst) in enumerate(
            ((old_hbm, old_v), (gain_hbm, gain_v), (new_hbm, new_v), (gl_hbm, gl_v), (ul_hbm, ul_v), (dr_hbm, dr_v))
        )
    ]
    for load in small:
        load.start()
    loads = [
        pltpu.make_async_copy(gate_hbm, w_in.at[0:FL], local_sem.at[0]),
        pltpu.make_async_copy(up_hbm, w_in.at[FL : 2 * FL], local_sem.at[1]),
        pltpu.make_async_copy(down_hbm, down_v, local_sem.at[2]),
        pltpu.make_async_copy(gr_hbm, gr_v, local_sem.at[3]),
        pltpu.make_async_copy(ur_hbm, ur_v, local_sem.at[4]),
        pltpu.make_async_copy(dl_hbm, dl_v, local_sem.at[5]),
    ]
    for load in loads:
        load.start()

    lane = lax.broadcasted_iota(jnp.int32, (OWN, LANES), 1)
    sums = jnp.zeros((OWN, LANES), F32)
    for load in small:
        load.wait()
    gain = gain_v[...]
    folded = []
    for i, ref in enumerate((old_v, new_v)):
        values = ref[...].astype(F32)
        square = jnp.sum(values * values, axis=1, keepdims=True)
        high = square.astype(BF16).astype(F32)
        sums = jnp.where(lane == 2 * i, high, sums)
        sums = jnp.where(lane == 2 * i + 1, square - high, sums)
        folded.append(fold(values * gain))
    zeros = jnp.zeros((48 - CHUNKS * OWN - OWN, LANES), F32)
    s1_old[0] = jnp.concatenate(folded[0] + [sums, zeros], axis=0).astype(BF16)
    s1_new[0] = jnp.concatenate(folded[1], axis=0).astype(BF16)
    left[c, y, zh] = jnp.concatenate([gl_v[...], ul_v[...]], axis=1)
    right[c, y, zh] = jnp.concatenate([dr_v[...], jnp.zeros((16, LANES - R), BF16)], axis=1)

    pl.semaphore_wait(barrier, len(greet))

    class Plane:
        def __init__(self, core):
            self.core = core
            first = (NZ, Z_ORDER, z_peer)
            second = (NY, Y_ORDER, y_peer)
            if core == 1:
                first, second = second, first
            self.n1, self.order1, self.peer1 = first
            self.n2, self.order2, self.peer2 = second
            self.rows = OWN * self.n1

        def block(self, k):
            return pl.ds(k * self.rows, self.rows)

    planes = (Plane(0), Plane(1))
    base = {}
    for name in ("a1o", "a1n", "a1l", "a1r", "a2o", "a2n", "a2l", "a2r", "fo", "fn", "c1o", "c1n", "c2o", "c2n", "to", "tn", "tl", "ho", "hn"):
        base[name] = sems(8)
    for name in ("fl", "fr", "eo", "en"):
        base[name] = sems(1)

    def a1_copies(pln, name, s1):
        return [remote(s1.at[0], s1.at[k], base[name] + k, base[name] + k, pln.peer1(k)) for k in pln.order1]

    def a1_factor_copies(pln, name, fac):
        own = fac.at[c, y, zh]
        return [remote(own, own, base[name] + k, base[name] + k, z_peer(k)) for k in Z_ORDER]

    def a2_copies(pln, name, x_ref):
        return [
            remote(x_ref.at[0, pln.block(0)], x_ref.at[0, pln.block(k)], base[name] + k, base[name] + k, pln.peer2(k))
            for k in pln.order2
        ]

    def a2_factor_copies(pln, name, fac):
        part = fac.at[c, y]
        return [remote(part, part, base[name] + k, base[name] + k, y_peer(k)) for k in Y_ORDER]

    def forward(pln, name, x_ref, k):
        return remote(x_ref.at[0, pln.block(k)], x_ref.at[1, pln.block(k)], base[name] + k, base[name], sibling)

    def assemble(pln, s1, x_ref, chunks):
        parts = [s1[k].astype(F32) for k in range(pln.n1)]
        for j in range(chunks):
            tile = jnp.concatenate([part[OWN * j : OWN * (j + 1)] for part in parts], axis=0)
            x_ref[0, 0 : pln.rows, j * LANES : (j + 1) * LANES] = tile.astype(BF16)

    def per_core(fn):
        for pln in planes:
            pl.when(c == pln.core)(functools.partial(fn, pln))

    def gather_first(pln):
        olds, news = a1_copies(pln, "a1o", s1_old), a1_copies(pln, "a1n", s1_new)
        lefts, rights = a1_factor_copies(pln, "a1l", left), a1_factor_copies(pln, "a1r", right)
        seconds = a2_copies(pln, "a2o", x_old)
        for copy in olds + news:
            copy.start()
        for copy in olds:
            copy.wait_recv()
        assemble(pln, s1_old, x_old, CHUNKS + 1)
        for copy in seconds:
            copy.start()
        forward(pln, "fo", x_old, 0).start()
        for copy in lefts + rights:
            copy.start()
        for copy in news:
            copy.wait_recv()
        assemble(pln, s1_new, x_new, CHUNKS)
        for copy in seconds:
            copy.wait_send()
        for copy in a2_copies(pln, "a2n", x_new):
            copy.start()
        forward(pln, "fn", x_new, 0).start()

    per_core(gather_first)
    for load in loads:
        load.wait()

    def gather_second(pln, name, forward_name, x_ref):
        copies = a2_copies(pln, name, x_ref)
        for k, copy in reversed(list(zip(pln.order2, copies))):
            copy.wait_recv()
            forward(pln, forward_name, x_ref, k).start()

    def wait_sibling_half(name, x_ref):
        remote(x_ref.at[0], x_ref.at[1], base[name], base[name], sibling).wait_recv()

    def reduce_copy(name, p_ref, t_ref, b):
        return remote(p_ref.at[b], t_ref.at[pos], base[name] + b, base[name] + pos, (g, block_target(b)))

    def project(half, x_ref, p_ref, t_ref, name, with_sums):
        product = lax.dot_general(
            x_ref[half, :, 0:DL], w_in[...], (((1,), (1,)), ((), ())), preferred_element_type=F32
        )
        p_ref[4 * half : 4 * half + 4, :, 0 : 2 * FL] = product.astype(BF16).reshape(4, BLOCK, 2 * FL)
        if with_sums:
            p_ref[4 * half : 4 * half + 4, :, 2 * FL :] = x_ref[half, :, DL:].reshape(4, BLOCK, LANES)
        for b in range(4 * half, 4 * half + 4):
            pl.when(b != pos)(lambda b=b: reduce_copy(name, p_ref, t_ref, b).start())

    def reduced(p_ref, t_ref, name):
        t_ref[pos] = p_ref[pos]
        for b in range(NT):
            def wait(b=b):
                remote(p_ref.at[b], t_ref.at[b], base[name] + b, base[name] + b, (g, block_target(b))).wait_recv()
            pl.when(b != pos)(wait)
        total = t_ref[0].astype(F32)
        for b in range(1, NT):
            total += t_ref[b].astype(F32)
        return total

    def hidden_copies(name, h_ref):
        copies = []
        for k in (6, 2, 5, 3, 7, 1, 4):
            b = (pos + k) % NT
            copies.append(remote(h_ref.at[pos], h_ref.at[pos], base[name] + b, base[name] + pos, (g, block_target(b))))
        return copies

    def activate(gate, up, h_ref):
        h_ref[pos] = (gate / (1.0 + jnp.exp(-gate)) * up).astype(BF16)

    def spread(name, h_ref):
        for copy in hidden_copies(name, h_ref):
            copy.start()

    def wait_hidden(name, h_ref, half):
        for b in range(4 * half, 4 * half + 4):
            def wait(b=b):
                remote(h_ref.at[b], h_ref.at[b], base[name] + b, base[name] + b, (g, block_target(b))).wait_recv()
            pl.when(b != pos)(wait)

    def down_project(h_name, h_ref, down_ref, d_sib, e_ref, e_name, cs_ref):
        wait_hidden(h_name, h_ref, 1)
        d_sib[...] = jnp.dot(
            h_ref[4:8].reshape(HALF, FL), down_ref[...], preferred_element_type=F32
        ).astype(BF16)
        exchange = remote(d_sib, e_ref, base[e_name], base[e_name], sibling)
        exchange.start()
        wait_hidden(h_name, h_ref, 0)
        d_own[...] = jnp.dot(h_ref[0:4].reshape(HALF, FL), down_ref[...], preferred_element_type=F32)
        exchange.wait_recv()
        d_own[...] += e_ref[...].astype(F32)
        cs_ref[...] = d_own[...].astype(BF16)

    def c1_copies(pln, name, cs_ref, r1_ref):
        return [
            remote(cs_ref.at[pln.block(k)], r1_ref.at[pln.block(k)], base[name] + k, base[name] + k, pln.peer2(-k))
            for k in pln.order2
        ]

    def c2_copies(pln, name, c2_ref, r2_ref):
        return [
            remote(c2_ref.at[k], r2_ref.at[k], base[name] + k, base[name] + k, pln.peer1(-k)) for k in pln.order1
        ]

    def scatter_first(pln, name, cs_ref, r1_ref):
        for copy in c1_copies(pln, name, cs_ref, r1_ref):
            copy.start()

    def scatter_second(pln, name1, cs_ref, r1_ref, name2, c2_ref, r2_ref):
        for copy in c1_copies(pln, name1, cs_ref, r1_ref):
            copy.wait_recv()
        total = cs_ref[pln.block(0)].astype(F32)
        for k in range(1, pln.n2):
            total += r1_ref[pln.block(k)].astype(F32)
        for k in range(pln.n1):
            piece = jnp.concatenate(fold(total[OWN * k : OWN * (k + 1)]), axis=0)
            c2_ref[k] = piece.astype(BF16)
        for copy in c2_copies(pln, name2, c2_ref, r2_ref):
            copy.start()

    def scatter_last(pln, name2, c2_ref, r2_ref, out_ref):
        for copy in c2_copies(pln, name2, c2_ref, r2_ref):
            copy.wait_recv()
        total = c2_ref[0].astype(F32)
        for k in range(1, pln.n1):
            total += r2_ref[k].astype(F32)
        out_ref[...] = jnp.concatenate(
            [total[OWN * j : OWN * (j + 1)] for j in range(CHUNKS)], axis=1
        ).astype(BF16)

    per_core(lambda pln: gather_second(pln, "a2o", "fo", x_old))
    project(0, x_old, p_old, t_old, "to", True)
    wait_sibling_half("fo", x_old)
    project(1, x_old, p_old, t_old, "to", True)

    def gather_rest(pln):
        gather_second(pln, "a2n", "fn", x_new)
        for copy in a2_copies(pln, "a2n", x_new):
            copy.wait_send()
        for name1, name2, fac in (("a1l", "a2l", left), ("a1r", "a2r", right)):
            for copy in a1_factor_copies(pln, name1, fac):
                copy.wait_recv()
            for copy in a2_factor_copies(pln, name2, fac):
                copy.start()

    per_core(gather_rest)
    for b in range(NT):
        pl.when(b != pos)(lambda b=b: reduce_copy("to", p_old, t_old, b).wait_send())
    project(0, x_new, p_new, t_new, "tn", False)
    wait_sibling_half("fn", x_new)
    project(1, x_new, p_new, t_new, "tn", False)

    total = reduced(p_old, t_old, "to")
    mean = total[:, 2 * FL :] * (1.0 / D)
    inverse_old = lax.rsqrt(mean[:, 0:1] + mean[:, 1:2] + 1e-05)
    inv_new[...] = jnp.broadcast_to(lax.rsqrt(mean[:, 2:3] + mean[:, 3:4] + 1e-05), (BLOCK, LANES))
    activate(total[:, 0:FL] * inverse_old, total[:, FL : 2 * FL] * inverse_old, h_old)

    def exchange_factors(name2, name, fac):
        def wait(pln):
            for copy in a2_factor_copies(pln, name2, fac):
                copy.wait_recv()

        per_core(wait)
        copy = remote(fac.at[c], fac.at[c], base[name], base[name], sibling)
        copy.start()
        return copy

    left_exchange = exchange_factors("a2l", "fl", left)
    left_exchange.wait_recv()
    low = jnp.zeros((ROWS, 2 * R), F32)
    for q in range(NZ):
        part = jnp.concatenate([left[i % 2, i // 2, q] for i in range(2 * NY)], axis=0)
        columns = x_new[:, :, q * 256 : (q + 1) * 256].reshape(ROWS, 256)
        low += jnp.dot(columns, part, preferred_element_type=F32)
    p_low[...] = low.astype(BF16).reshape(NT, BLOCK, 2 * R)
    for b in range(NT):
        pl.when(b != pos)(lambda b=b: reduce_copy("tl", p_low, t_low, b).start())
    right_exchange = exchange_factors("a2r", "fr", right)

    for b in range(NT):
        pl.when(b != pos)(lambda b=b: reduce_copy("tn", p_new, t_new, b).wait_send())
    spread("ho", h_old)

    total = reduced(p_new, t_new, "tn")
    low = reduced(p_low, t_low, "tl").astype(BF16)
    gate = total[:, 0:FL] + ALPHA / R * jnp.dot(low[:, 0:R], gr_v[...], preferred_element_type=F32)
    up = total[:, FL : 2 * FL] + ALPHA / R * jnp.dot(low[:, R : 2 * R], ur_v[...], preferred_element_type=F32)
    activate(gate * inv_new[:, 0:1], up * inv_new[:, 0:1], h_new)
    spread("hn", h_new)
    right_exchange.wait_recv()
    for q in range(NZ):
        columns = pl.ds(q * 256, 256)
        part = jnp.concatenate([right[i % 2, i // 2, q, :, 0:R] for i in range(2 * NY)], axis=0)
        product = lax.dot_general(dl_v[...], part, (((0,), (1,)), ((), ())), preferred_element_type=F32)
        down_new[:, columns] = (down_v[:, columns].astype(F32) + ALPHA / R * product).astype(BF16)

    down_project("ho", h_old, down_v, d_sib_old, e_old, "eo", cs_old)
    per_core(lambda pln: scatter_first(pln, "c1o", cs_old, r1_old))

    down_project("hn", h_new, down_new, d_sib_new, e_new, "en", cs_new)
    per_core(lambda pln: scatter_first(pln, "c1n", cs_new, r1_new))
    per_core(lambda pln: scatter_second(pln, "c1o", cs_old, r1_old, "c2o", c2_old, r2_old))
    per_core(lambda pln: scatter_second(pln, "c1n", cs_new, r1_new, "c2n", c2_new, r2_new))
    per_core(lambda pln: scatter_last(pln, "c2o", c2_old, r2_old, out_old_ref))
    per_core(lambda pln: scatter_last(pln, "c2n", c2_new, r2_new, out_new_ref))

    def drain(pln):
        copies = a1_copies(pln, "a1o", s1_old) + a1_copies(pln, "a1n", s1_new)
        copies += a1_factor_copies(pln, "a1l", left) + a1_factor_copies(pln, "a1r", right)
        copies += a2_factor_copies(pln, "a2l", left) + a2_factor_copies(pln, "a2r", right)
        copies += [forward(pln, "fo", x_old, k) for k in range(pln.n2)]
        copies += [forward(pln, "fn", x_new, k) for k in range(pln.n2)]
        copies += c1_copies(pln, "c1o", cs_old, r1_old) + c1_copies(pln, "c1n", cs_new, r1_new)
        copies += c2_copies(pln, "c2o", c2_old, r2_old) + c2_copies(pln, "c2n", c2_new, r2_new)
        for copy in copies:
            copy.wait_send()

    per_core(drain)
    left_exchange.wait_send()
    right_exchange.wait_send()
    remote(d_sib_old, e_old, base["eo"], base["eo"], sibling).wait_send()
    remote(d_sib_new, e_new, base["en"], base["en"], sibling).wait_send()
    for b in range(NT):
        def wait(b=b):
            reduce_copy("tl", p_low, t_low, b).wait_send()
        pl.when(b != pos)(wait)
    for copy in hidden_copies("ho", h_old) + hidden_copies("hn", h_new):
        copy.wait_send()


def per_device(old, new, gain, gate, up, down, gl, gr, ul, ur, dl, dr):
    vmem = pl.BlockSpec(memory_space=pltpu.VMEM)
    hbm = pl.BlockSpec(memory_space=pl.ANY)
    scratch = [
        ((OWN, DL), BF16), ((OWN, DL), BF16), ((1, DL), F32),
        ((16, R), BF16), ((16, R), BF16), ((16, R), BF16),
        ((R, FL), BF16), ((R, FL), BF16), ((R, FL), BF16),
        ((2 * FL, DL), BF16), ((FL, DL), BF16), ((FL, DL), BF16),
        ((8, 48, LANES), BF16), ((8, 32, LANES), BF16),
        ((2, NY, NZ, 16, LANES), BF16), ((2, NY, NZ, 16, LANES), BF16),
        ((2, HALF, DL + LANES), BF16), ((2, HALF, DL), BF16),
        ((NT, BLOCK, 2 * FL + LANES), BF16), ((NT, BLOCK, 2 * FL), BF16), ((NT, BLOCK, 2 * R), BF16),
        ((NT, BLOCK, 2 * FL + LANES), BF16), ((NT, BLOCK, 2 * FL), BF16), ((NT, BLOCK, 2 * R), BF16),
        ((NT, BLOCK, FL), BF16), ((NT, BLOCK, FL), BF16),
        ((HALF, DL), F32), ((HALF, DL), BF16), ((HALF, DL), BF16),
        ((HALF, DL), BF16), ((HALF, DL), BF16), ((HALF, DL), BF16), ((HALF, DL), BF16),
        ((HALF, DL), BF16), ((HALF, DL), BF16),
        ((8, 32, LANES), BF16), ((8, 32, LANES), BF16), ((8, 32, LANES), BF16), ((8, 32, LANES), BF16),
        ((BLOCK, LANES), F32),
    ]
    flops = 2 * (2 * ROWS * DL * FL * 3 + 3 * DL * FL * R)
    return pl.pallas_call(
        kernel,
        out_shape=[jax.ShapeDtypeStruct((OWN, DL), BF16)] * 2,
        in_specs=[hbm] * 12,
        out_specs=[vmem, vmem],
        scratch_shapes=[pltpu.VMEM(shape, dtype) for shape, dtype in scratch]
        + [pltpu.SemaphoreType.DMA((12,)), pltpu.SemaphoreType.DMA((156,)), pltpu.SemaphoreType.DMA((156,))],
        compiler_params=pltpu.CompilerParams(
            collective_id=0, has_side_effects=True, vmem_limit_bytes=60 * 1024 * 1024
        ),
        cost_estimate=pl.CostEstimate(flops=flops, bytes_accessed=6 * DL * FL, transcendentals=2 * BLOCK * FL),
    )(old, new, gain.reshape(1, DL), gl, ul, dr, gr, ur, dl.T, gate.T, up.T, down)


def solution(mesh):
    in_specs = (
        P("groups", "tensor"),
        P("groups", "tensor"),
        P("tensor"),
        P("tensor", "groups"),
        P("tensor", "groups"),
        P("groups", "tensor"),
        P(("tensor", "groups"), None),
        P(None, "groups"),
        P(("tensor", "groups"), None),
        P(None, "groups"),
        P("groups", None),
        P(("tensor", "groups"), None),
    )
    out_specs = (P("groups", "tensor"), P("groups", "tensor"))
    return jax.shard_map(per_device, mesh=mesh, in_specs=in_specs, out_specs=out_specs, check_vma=False)
```

```python
import functools

import jax
import jax.numpy as jnp
from jax import lax
from jax.experimental import pallas as pl
from jax.experimental.pallas import tpu as pltpu
from jax.sharding import PartitionSpec as P

MESH = pl.DeviceIdType.MESH
F32, BF16 = jnp.float32, jnp.bfloat16
D = 8192
R = 64
ALPHA = 32
NZ, NY, NT = 4, 8, 8
DL, FL = 1024, 448
ROWS, OWN = 256, 4
HALF = ROWS // 2
BLOCK = ROWS // NT
PIECE = HALF // 2
LANES = 128
CHUNKS = DL // LANES
Z_ORDER = (2, 1, 3)
Y_ORDER = (4, 3, 5, 2, 6, 1, 7)


def block_target(b):
    x = b % 4
    return x * 2 + (b // 4 + x) % 2


def fold(values):
    return [values[:, j * LANES : (j + 1) * LANES] for j in range(CHUNKS)]


def kernel(
    old_hbm, new_hbm, gain_hbm, gl_hbm, ul_hbm, dr_hbm, gr_hbm, ur_hbm, dl_hbm, gate_hbm, up_hbm, down_hbm,
    out_old_ref, out_new_ref,
    old_v, new_v, gain_v, gl_v, ul_v, dr_v, gr_v, ur_v, dl_v, w_in, down_v, down_new,
    s1_old, s1_new, left, right, x_old, x_new,
    p_old, p_new, p_low, t_old, t_new, t_low, h_old, h_new,
    d_sib_old, d_sib_new, e_old, e_new, cs_old, cs_new, r1_old, r1_new, c2_old, c2_new, r2_old, r2_new, square,
    local_sem, ss, rs,
):
    g, t = lax.axis_index("groups"), lax.axis_index("tensor")
    zh, y, c = g // 16, (g // 2) % 8, g % 2
    pos = (t // 2) + 4 * ((t % 2 + t // 2) % 2)
    sibling = (zh * 16 + y * 2 + (1 - c), t)

    def z_peer(k):
        return (((zh + k) % NZ) * 16 + y * 2 + c, t)

    def y_peer(k):
        return (zh * 16 + ((y + k) % NY) * 2 + c, t)

    counter = [0]

    def sems(n):
        counter[0] += n
        return counter[0] - n

    def remote(src, dst, s, r, dev):
        return pltpu.make_async_remote_copy(
            src_ref=src, dst_ref=dst, send_sem=ss.at[s], recv_sem=rs.at[r], device_id=dev, device_id_type=MESH
        )

    barrier = pltpu.get_barrier_semaphore()
    greet = [sibling] + [z_peer(k) for k in Z_ORDER] + [y_peer(k) for k in Y_ORDER]
    greet += [(g, (t + k) % NT) for k in range(1, NT)]
    for dev in greet:
        pl.semaphore_signal(barrier, inc=1, device_id=dev, device_id_type=MESH)

    small = [
        pltpu.make_async_copy(src, dst, local_sem.at[6 + n])
        for n, (src, dst) in enumerate(
            ((old_hbm, old_v), (gain_hbm, gain_v), (new_hbm, new_v), (gl_hbm, gl_v), (ul_hbm, ul_v), (dr_hbm, dr_v))
        )
    ]
    for load in small:
        load.start()
    loads = [
        pltpu.make_async_copy(gate_hbm, w_in.at[0:FL], local_sem.at[0]),
        pltpu.make_async_copy(up_hbm, w_in.at[FL : 2 * FL], local_sem.at[1]),
        pltpu.make_async_copy(down_hbm, down_v, local_sem.at[2]),
        pltpu.make_async_copy(gr_hbm, gr_v, local_sem.at[3]),
        pltpu.make_async_copy(ur_hbm, ur_v, local_sem.at[4]),
        pltpu.make_async_copy(dl_hbm, dl_v, local_sem.at[5]),
    ]
    for load in loads:
        load.start()

    def scaled(ref):
        return fold(ref[...].astype(F32) * gain_v[...])

    for load in small[:3]:
        load.wait()
    s1_old[0] = jnp.concatenate(scaled(old_v), axis=0).astype(BF16)
    lane = lax.broadcasted_iota(jnp.int32, (OWN, LANES), 1)
    squares = [jnp.sum(ref[...].astype(F32) ** 2, axis=1, keepdims=True) for ref in (old_v, new_v)]
    squares = jnp.where(lane == 0, squares[0], jnp.where(lane == 1, squares[1], 0.0))
    square[pos] = jnp.concatenate([squares, jnp.zeros((8 - OWN, LANES), F32)], axis=0)

    pl.semaphore_wait(barrier, len(greet))

    class Plane:
        def __init__(self, core):
            self.core = core
            first = (NZ, Z_ORDER, z_peer)
            second = (NY, Y_ORDER, y_peer)
            if core == 1:
                first, second = second, first
            self.n1, self.order1, self.peer1 = first
            self.n2, self.order2, self.peer2 = second
            self.rows = OWN * self.n1

        def block(self, k):
            return pl.ds(k * self.rows, self.rows)

    planes = (Plane(0), Plane(1))
    base = {}
    for name in ("a1o", "a1n", "a1l", "a1r", "a2o", "a2n", "a2l", "a2r", "fo", "fn", "c1o", "c1n", "c2o", "c2n", "to", "tn", "tl", "ho", "hn", "sq"):
        base[name] = sems(8)
    for name in ("fl", "fr", "eo", "en"):
        base[name] = sems(2)

    def a1_copies(pln, name, s1):
        return [remote(s1.at[0], s1.at[k], base[name] + k, base[name] + k, pln.peer1(k)) for k in pln.order1]

    def a1_factor_copies(pln, name, fac):
        own = fac.at[c, y, zh]
        return [remote(own, own, base[name] + k, base[name] + k, z_peer(k)) for k in Z_ORDER]

    def a2_copies(pln, name, x_ref):
        return [
            remote(x_ref.at[0, pln.block(0)], x_ref.at[0, pln.block(k)], base[name] + k, base[name] + k, pln.peer2(k))
            for k in pln.order2
        ]

    def a2_factor_copies(pln, name, fac):
        part = fac.at[c, y]
        return [remote(part, part, base[name] + k, base[name] + k, y_peer(k)) for k in Y_ORDER]

    def forward(pln, name, x_ref, k):
        return remote(x_ref.at[0, pln.block(k)], x_ref.at[1, pln.block(k)], base[name] + k, base[name], sibling)

    def assemble(pln, s1, x_ref, chunks):
        parts = [s1[k].astype(F32) for k in range(pln.n1)]
        for j in range(chunks):
            tile = jnp.concatenate([part[OWN * j : OWN * (j + 1)] for part in parts], axis=0)
            x_ref[0, 0 : pln.rows, j * LANES : (j + 1) * LANES] = tile.astype(BF16)

    def per_core(fn):
        for pln in planes:
            pl.when(c == pln.core)(functools.partial(fn, pln))

    def hidden_copies(name, h_ref):
        copies = []
        for k in (6, 2, 5, 3, 7, 1, 4):
            b = (pos + k) % NT
            copies.append(remote(h_ref.at[pos], h_ref.at[pos], base[name] + b, base[name] + pos, (g, block_target(b))))
        return copies

    def wait_hidden(name, h_ref, blocks):
        for b in blocks:
            def wait(b=b):
                remote(h_ref.at[b], h_ref.at[b], base[name] + b, base[name] + b, (g, block_target(b))).wait_recv()
            pl.when(b != pos)(wait)

    def gather_first(pln):
        olds, news = a1_copies(pln, "a1o", s1_old), a1_copies(pln, "a1n", s1_new)
        lefts, rights = a1_factor_copies(pln, "a1l", left), a1_factor_copies(pln, "a1r", right)
        seconds = a2_copies(pln, "a2o", x_old)
        for copy in olds + hidden_copies("sq", square):
            copy.start()
        s1_new[0] = jnp.concatenate(scaled(new_v), axis=0).astype(BF16)
        for copy in news:
            copy.start()
        for load in small[3:]:
            load.wait()
        left[c, y, zh] = jnp.concatenate([gl_v[...], ul_v[...]], axis=1)
        for copy in olds:
            copy.wait_recv()
        assemble(pln, s1_old, x_old, CHUNKS)
        for copy in seconds:
            copy.start()
        forward(pln, "fo", x_old, 0).start()
        for copy in lefts:
            copy.start()
        wait_hidden("sq", square, range(NT))
        total = square[0]
        for b in range(1, NT):
            total += square[b]
        inverse = lax.rsqrt(total * (1.0 / D) + 1e-05)
        high = inverse.astype(BF16).astype(F32)
        low = inverse - high
        lane = lax.broadcasted_iota(jnp.int32, (8, LANES - R), 1)
        beside = jnp.zeros((8, LANES - R), F32)
        for n, column in enumerate((high[:, 0:1], low[:, 0:1], high[:, 1:2], low[:, 1:2])):
            beside = jnp.where(lane == n, column, beside)
        beside = jnp.concatenate([beside, jnp.zeros((8, LANES - R), F32)], axis=0)
        right[c, y, zh] = jnp.concatenate([dr_v[...].astype(F32), beside], axis=1).astype(BF16)
        for copy in rights:
            copy.start()
        for copy in news:
            copy.wait_recv()
        assemble(pln, s1_new, x_new, CHUNKS)
        for copy in seconds:
            copy.wait_send()
        for copy in a2_copies(pln, "a2n", x_new):
            copy.start()
        forward(pln, "fn", x_new, 0).start()

    per_core(gather_first)
    for load in loads:
        load.wait()

    def gather_second(pln, name, forward_name, x_ref):
        copies = a2_copies(pln, name, x_ref)
        for k, copy in reversed(list(zip(pln.order2, copies))):
            copy.wait_recv()
            forward(pln, forward_name, x_ref, k).start()

    def wait_sibling_half(name, x_ref):
        remote(x_ref.at[0], x_ref.at[1], base[name], base[name], sibling).wait_recv()

    def reduce_copy(name, p_ref, t_ref, b):
        return remote(p_ref.at[b], t_ref.at[pos], base[name] + b, base[name] + pos, (g, block_target(b)))

    def project(half, x_ref, p_ref, t_ref, name):
        product = lax.dot_general(
            x_ref[half, :, 0:DL], w_in[...], (((1,), (1,)), ((), ())), preferred_element_type=F32
        )
        p_ref[4 * half : 4 * half + 4, :, 0 : 2 * FL] = product.astype(BF16).reshape(4, BLOCK, 2 * FL)
        for b in range(4 * half, 4 * half + 4):
            pl.when(b != pos)(lambda b=b: reduce_copy(name, p_ref, t_ref, b).start())

    def reduced(p_ref, t_ref, name):
        t_ref[pos] = p_ref[pos]
        for b in range(NT):
            def wait(b=b):
                remote(p_ref.at[b], t_ref.at[b], base[name] + b, base[name] + b, (g, block_target(b))).wait_recv()
            pl.when(b != pos)(wait)
        total = t_ref[0].astype(F32)
        for b in range(1, NT):
            total += t_ref[b].astype(F32)
        return total

    def activate(gate, up, h_ref):
        h_ref[pos] = (gate / (1.0 + jnp.exp(-gate)) * up).astype(BF16)

    def spread(name, h_ref):
        for copy in hidden_copies(name, h_ref):
            copy.start()

    def c1_copies(pln, name, cs_ref, r1_ref):
        return [
            remote(cs_ref.at[pln.block(k)], r1_ref.at[pln.block(k)], base[name] + k, base[name] + k, pln.peer2(-k))
            for k in pln.order2
        ]

    def c2_copies(pln, name, c2_ref, r2_ref):
        return [
            remote(c2_ref.at[k], r2_ref.at[k], base[name] + k, base[name] + k, pln.peer1(-k)) for k in pln.order1
        ]

    def exchange_piece(name, d_sib, e_ref, piece):
        rows = pl.ds(piece * PIECE, PIECE)
        return remote(d_sib.at[rows], e_ref.at[rows], base[name] + piece, base[name] + piece, sibling)

    def down_project(h_name, h_ref, down_ref, d_sib, e_ref, e_name, cs_ref, c1_name, r1_ref):
        def product(half, piece):
            first = 4 * half + 2 * piece
            wait_hidden(h_name, h_ref, (first, first + 1))
            return jnp.dot(
                h_ref[first : first + 2].reshape(PIECE, FL), down_ref[...], preferred_element_type=F32
            )

        for piece in (1, 0):
            d_sib[piece * PIECE : (piece + 1) * PIECE] = product(1, piece).astype(BF16)
            exchange_piece(e_name, d_sib, e_ref, piece).start()
        for piece in (1, 0):
            rows = pl.ds(piece * PIECE, PIECE)
            own = product(0, piece)
            exchange_piece(e_name, d_sib, e_ref, piece).wait_recv()
            cs_ref[rows] = (own + e_ref[rows].astype(F32)).astype(BF16)

            def start(pln, piece=piece):
                n = PIECE // pln.rows
                for k, copy in zip(pln.order2, c1_copies(pln, c1_name, cs_ref, r1_ref)):
                    if k // n == piece:
                        copy.start()

            per_core(start)

    def scatter_second(pln, name1, cs_ref, r1_ref, name2, c2_ref, r2_ref):
        for copy in c1_copies(pln, name1, cs_ref, r1_ref):
            copy.wait_recv()
        total = cs_ref[pln.block(0)].astype(F32)
        for k in range(1, pln.n2):
            total += r1_ref[pln.block(k)].astype(F32)
        for k in range(pln.n1):
            piece = jnp.concatenate(fold(total[OWN * k : OWN * (k + 1)]), axis=0)
            c2_ref[k] = piece.astype(BF16)
        for copy in c2_copies(pln, name2, c2_ref, r2_ref):
            copy.start()

    def scatter_last(pln, name2, c2_ref, r2_ref, out_ref):
        for copy in c2_copies(pln, name2, c2_ref, r2_ref):
            copy.wait_recv()
        total = c2_ref[0].astype(F32)
        for k in range(1, pln.n1):
            total += r2_ref[k].astype(F32)
        out_ref[...] = jnp.concatenate(
            [total[OWN * j : OWN * (j + 1)] for j in range(CHUNKS)], axis=1
        ).astype(BF16)

    per_core(lambda pln: gather_second(pln, "a2o", "fo", x_old))
    project(0, x_old, p_old, t_old, "to")
    wait_sibling_half("fo", x_old)
    project(1, x_old, p_old, t_old, "to")

    def gather_rest(pln):
        gather_second(pln, "a2n", "fn", x_new)
        for copy in a2_copies(pln, "a2n", x_new):
            copy.wait_send()
        for name1, name2, fac in (("a1l", "a2l", left), ("a1r", "a2r", right)):
            for copy in a1_factor_copies(pln, name1, fac):
                copy.wait_recv()
            for copy in a2_factor_copies(pln, name2, fac):
                copy.start()

    per_core(gather_rest)
    for b in range(NT):
        pl.when(b != pos)(lambda b=b: reduce_copy("to", p_old, t_old, b).wait_send())
    project(0, x_new, p_new, t_new, "tn")
    wait_sibling_half("fn", x_new)
    project(1, x_new, p_new, t_new, "tn")

    def exchange_factors(name2, name, fac):
        def wait(pln):
            for copy in a2_factor_copies(pln, name2, fac):
                copy.wait_recv()

        per_core(wait)
        copy = remote(fac.at[c], fac.at[c], base[name], base[name], sibling)
        copy.start()
        return copy

    left_exchange = exchange_factors("a2l", "fl", left)
    left_exchange.wait_recv()
    low = jnp.zeros((ROWS, 2 * R), F32)
    for q in range(NZ):
        part = jnp.concatenate([left[i % 2, i // 2, q] for i in range(2 * NY)], axis=0)
        columns = x_new[:, :, q * 256 : (q + 1) * 256].reshape(ROWS, 256)
        low += jnp.dot(columns, part, preferred_element_type=F32)
    p_low[...] = low.astype(BF16).reshape(NT, BLOCK, 2 * R)
    for b in range(NT):
        pl.when(b != pos)(lambda b=b: reduce_copy("tl", p_low, t_low, b).start())
    right_exchange = exchange_factors("a2r", "fr", right)

    total = reduced(p_old, t_old, "to")
    right_exchange.wait_recv()
    core, i = c + (1 - 2 * c) * (pos // 4), pos % 4
    rows = []
    for n in range(8):
        ky = (1 - core) * (2 * i + n // 4) + core * n
        kz = (1 - core) * (n % 4) + core * i
        rows.append(right[core, (y - ky + NY) % NY, (zh - kz + NZ) % NZ].astype(F32)[0:OWN])
    inverse = jnp.concatenate(rows, axis=0)
    inverse_old = inverse[:, R : R + 1] + inverse[:, R + 1 : R + 2]
    inverse_new = inverse[:, R + 2 : R + 3] + inverse[:, R + 3 : R + 4]
    activate(total[:, 0:FL] * inverse_old, total[:, FL : 2 * FL] * inverse_old, h_old)

    for b in range(NT):
        pl.when(b != pos)(lambda b=b: reduce_copy("tn", p_new, t_new, b).wait_send())
    spread("ho", h_old)

    total = reduced(p_new, t_new, "tn")
    low = reduced(p_low, t_low, "tl").astype(BF16)
    gate = total[:, 0:FL] + ALPHA / R * jnp.dot(low[:, 0:R], gr_v[...], preferred_element_type=F32)
    up = total[:, FL : 2 * FL] + ALPHA / R * jnp.dot(low[:, R : 2 * R], ur_v[...], preferred_element_type=F32)
    activate(gate * inverse_new, up * inverse_new, h_new)
    spread("hn", h_new)
    for q in range(NZ):
        columns = pl.ds(q * 256, 256)
        part = jnp.concatenate([right[i % 2, i // 2, q, :, 0:R] for i in range(2 * NY)], axis=0)
        product = lax.dot_general(dl_v[...], part, (((0,), (1,)), ((), ())), preferred_element_type=F32)
        down_new[:, columns] = (down_v[:, columns].astype(F32) + ALPHA / R * product).astype(BF16)

    down_project("ho", h_old, down_v, d_sib_old, e_old, "eo", cs_old, "c1o", r1_old)

    down_project("hn", h_new, down_new, d_sib_new, e_new, "en", cs_new, "c1n", r1_new)
    per_core(lambda pln: scatter_second(pln, "c1o", cs_old, r1_old, "c2o", c2_old, r2_old))
    per_core(lambda pln: scatter_second(pln, "c1n", cs_new, r1_new, "c2n", c2_new, r2_new))
    per_core(lambda pln: scatter_last(pln, "c2o", c2_old, r2_old, out_old_ref))

    def drain(pln):
        copies = a1_copies(pln, "a1o", s1_old) + a1_copies(pln, "a1n", s1_new)
        copies += a1_factor_copies(pln, "a1l", left) + a1_factor_copies(pln, "a1r", right)
        copies += a2_factor_copies(pln, "a2l", left) + a2_factor_copies(pln, "a2r", right)
        copies += [forward(pln, "fo", x_old, k) for k in range(pln.n2)]
        copies += [forward(pln, "fn", x_new, k) for k in range(pln.n2)]
        copies += c1_copies(pln, "c1o", cs_old, r1_old) + c1_copies(pln, "c1n", cs_new, r1_new)
        copies += c2_copies(pln, "c2o", c2_old, r2_old) + c2_copies(pln, "c2n", c2_new, r2_new)
        for copy in copies:
            copy.wait_send()

    per_core(drain)
    left_exchange.wait_send()
    right_exchange.wait_send()
    for piece in (1, 0):
        exchange_piece("eo", d_sib_old, e_old, piece).wait_send()
        exchange_piece("en", d_sib_new, e_new, piece).wait_send()
    for b in range(NT):
        def wait(b=b):
            reduce_copy("tl", p_low, t_low, b).wait_send()
        pl.when(b != pos)(wait)
    for copy in hidden_copies("sq", square) + hidden_copies("ho", h_old) + hidden_copies("hn", h_new):
        copy.wait_send()

    per_core(lambda pln: scatter_last(pln, "c2n", c2_new, r2_new, out_new_ref))


def hand_over(old_ref, new_ref, out_old_ref, out_new_ref, sem):
    copies = [
        pltpu.make_async_copy(old_ref, out_old_ref, sem.at[0]),
        pltpu.make_async_copy(new_ref, out_new_ref, sem.at[1]),
    ]
    for copy in copies:
        copy.start()
    for copy in copies:
        copy.wait()


def per_device(old, new, gain, gate, up, down, gl, gr, ul, ur, dl, dr):
    vmem = pl.BlockSpec(memory_space=pltpu.VMEM)
    hbm = pl.BlockSpec(memory_space=pl.ANY)
    scratch = [
        ((OWN, DL), BF16), ((OWN, DL), BF16), ((1, DL), F32),
        ((16, R), BF16), ((16, R), BF16), ((16, R), BF16),
        ((R, FL), BF16), ((R, FL), BF16), ((R, FL), BF16),
        ((2 * FL, DL), BF16), ((FL, DL), BF16), ((FL, DL), BF16),
        ((8, 32, LANES), BF16), ((8, 32, LANES), BF16),
        ((2, NY, NZ, 16, LANES), BF16), ((2, NY, NZ, 16, LANES), BF16),
        ((2, HALF, DL), BF16), ((2, HALF, DL), BF16),
        ((NT, BLOCK, 2 * FL), BF16), ((NT, BLOCK, 2 * FL), BF16), ((NT, BLOCK, 2 * R), BF16),
        ((NT, BLOCK, 2 * FL), BF16), ((NT, BLOCK, 2 * FL), BF16), ((NT, BLOCK, 2 * R), BF16),
        ((NT, BLOCK, FL), BF16), ((NT, BLOCK, FL), BF16),
        ((HALF, DL), BF16), ((HALF, DL), BF16),
        ((HALF, DL), BF16), ((HALF, DL), BF16), ((HALF, DL), BF16), ((HALF, DL), BF16),
        ((HALF, DL), BF16), ((HALF, DL), BF16),
        ((8, 32, LANES), BF16), ((8, 32, LANES), BF16), ((8, 32, LANES), BF16), ((8, 32, LANES), BF16),
        ((NT, 8, LANES), F32),
    ]
    flops = 2 * (2 * ROWS * DL * FL * 3 + 3 * DL * FL * R)
    out_shape = [jax.ShapeDtypeStruct((OWN, DL), BF16)] * 2
    outs = pl.pallas_call(
        kernel,
        out_shape=out_shape,
        in_specs=[hbm] * 12,
        out_specs=[vmem, vmem],
        scratch_shapes=[pltpu.VMEM(shape, dtype) for shape, dtype in scratch]
        + [pltpu.SemaphoreType.DMA((12,)), pltpu.SemaphoreType.DMA((168,)), pltpu.SemaphoreType.DMA((168,))],
        compiler_params=pltpu.CompilerParams(
            collective_id=0, has_side_effects=True, vmem_limit_bytes=60 * 1024 * 1024
        ),
        cost_estimate=pl.CostEstimate(flops=flops, bytes_accessed=6 * DL * FL, transcendentals=2 * BLOCK * FL),
    )(old, new, gain.reshape(1, DL), gl, ul, dr, gr, ur, dl.T, gate.T, up.T, down)
    return pl.pallas_call(
        hand_over,
        out_shape=out_shape,
        in_specs=[hbm, hbm],
        out_specs=[hbm, hbm],
        scratch_shapes=[pltpu.SemaphoreType.DMA((2,))],
    )(*outs)


def solution(mesh):
    in_specs = (
        P("groups", "tensor"),
        P("groups", "tensor"),
        P("tensor"),
        P("tensor", "groups"),
        P("tensor", "groups"),
        P("groups", "tensor"),
        P(("tensor", "groups"), None),
        P(None, "groups"),
        P(("tensor", "groups"), None),
        P(None, "groups"),
        P("groups", None),
        P(("tensor", "groups"), None),
    )
    out_specs = (P("groups", "tensor"), P("groups", "tensor"))
    return jax.shard_map(per_device, mesh=mesh, in_specs=in_specs, out_specs=out_specs, check_vma=False)
```

```python
import functools

import jax
import jax.numpy as jnp
from jax import lax
from jax.experimental import pallas as pl
from jax.experimental.pallas import tpu as pltpu
from jax.sharding import PartitionSpec as P

MESH = pl.DeviceIdType.MESH
F32, BF16 = jnp.float32, jnp.bfloat16
D = 8192
R = 64
ALPHA = 32
NZ, NY, NT = 4, 8, 8
DL, FL = 1024, 448
ROWS, OWN = 256, 4
HALF = ROWS // 2
BLOCK = ROWS // NT
PIECE = HALF // 2
LANES = 128
CHUNKS = DL // LANES
Z_ORDER = (2, 1, 3)
Y_ORDER = (4, 3, 5, 2, 6, 1, 7)


def block_target(b):
    x = b % 4
    return x * 2 + (b // 4 + x) % 2


def fold(values):
    return [values[:, j * LANES : (j + 1) * LANES] for j in range(CHUNKS)]


def kernel(
    old_hbm, new_hbm, gain_hbm, gl_hbm, ul_hbm, dr_hbm, gr_hbm, ur_hbm, dl_hbm, gate_hbm, up_hbm, down_hbm,
    out_old_ref, out_new_ref,
    old_v, new_v, gain_v, gl_v, ul_v, dr_v, gr_v, ur_v, dl_v, w_in, down_v, down_new,
    s1_old, s1_new, left, right, x_old, x_new,
    p_old, p_new, p_low, t_old, t_new, t_low, h_old, h_new,
    d_sib_old, d_sib_new, e_old, e_new, cs_old, cs_new, r1_old, r1_new, c2_old, c2_new, r2_old, r2_new, square,
    local_sem, ss, rs,
):
    g, t = lax.axis_index("groups"), lax.axis_index("tensor")
    zh, y, c = g // 16, (g // 2) % 8, g % 2
    pos = (t // 2) + 4 * ((t % 2 + t // 2) % 2)
    sibling = (zh * 16 + y * 2 + (1 - c), t)

    def z_peer(k):
        return (((zh + k) % NZ) * 16 + y * 2 + c, t)

    def y_peer(k):
        return (zh * 16 + ((y + k) % NY) * 2 + c, t)

    counter = [0]

    def sems(n):
        counter[0] += n
        return counter[0] - n

    def remote(src, dst, s, r, dev):
        return pltpu.make_async_remote_copy(
            src_ref=src, dst_ref=dst, send_sem=ss.at[s], recv_sem=rs.at[r], device_id=dev, device_id_type=MESH
        )

    barrier = pltpu.get_barrier_semaphore()
    greet = [sibling] + [z_peer(k) for k in Z_ORDER] + [y_peer(k) for k in Y_ORDER]
    greet += [(g, (t + k) % NT) for k in range(1, NT)]
    for dev in greet:
        pl.semaphore_signal(barrier, inc=1, device_id=dev, device_id_type=MESH)

    small = [
        pltpu.make_async_copy(src, dst, local_sem.at[6 + n])
        for n, (src, dst) in enumerate(
            ((old_hbm, old_v), (gain_hbm, gain_v), (new_hbm, new_v), (gl_hbm, gl_v), (ul_hbm, ul_v), (dr_hbm, dr_v))
        )
    ]
    for load in small:
        load.start()
    loads = [
        pltpu.make_async_copy(gate_hbm, w_in.at[0:FL], local_sem.at[0]),
        pltpu.make_async_copy(up_hbm, w_in.at[FL : 2 * FL], local_sem.at[1]),
        pltpu.make_async_copy(down_hbm, down_v, local_sem.at[2]),
        pltpu.make_async_copy(gr_hbm, gr_v, local_sem.at[3]),
        pltpu.make_async_copy(ur_hbm, ur_v, local_sem.at[4]),
        pltpu.make_async_copy(dl_hbm, dl_v, local_sem.at[5]),
    ]
    for load in loads:
        load.start()

    def scaled(ref):
        return fold(ref[...].astype(F32) * gain_v[...])

    for load in small[:3]:
        load.wait()
    s1_old[0] = jnp.concatenate(scaled(old_v), axis=0).astype(BF16)
    lane = lax.broadcasted_iota(jnp.int32, (OWN, LANES), 1)
    squares = [jnp.sum(ref[...].astype(F32) ** 2, axis=1, keepdims=True) for ref in (old_v, new_v)]
    squares = jnp.where(lane == 0, squares[0], jnp.where(lane == 1, squares[1], 0.0))
    square[pos] = jnp.concatenate([squares, jnp.zeros((8 - OWN, LANES), F32)], axis=0)

    pl.semaphore_wait(barrier, len(greet))

    class Plane:
        def __init__(self, core):
            self.core = core
            first = (NZ, Z_ORDER, z_peer)
            second = (NY, Y_ORDER, y_peer)
            if core == 1:
                first, second = second, first
            self.n1, self.order1, self.peer1 = first
            self.n2, self.order2, self.peer2 = second
            self.rows = OWN * self.n1

        def block(self, k):
            return pl.ds(k * self.rows, self.rows)

    planes = (Plane(0), Plane(1))
    base = {}
    for name in ("a1o", "a1n", "a1l", "a1r", "a2o", "a2n", "a2l", "a2r", "fo", "fn", "c1o", "c1n", "c2o", "c2n", "to", "tn", "tl", "ho", "hn", "sq"):
        base[name] = sems(8)
    for name in ("fl", "fr", "eo", "en"):
        base[name] = sems(2)

    def a1_copies(pln, name, s1):
        return [remote(s1.at[0], s1.at[k], base[name] + k, base[name] + k, pln.peer1(k)) for k in pln.order1]

    def a1_factor_copies(pln, name, fac):
        own = fac.at[c, y, zh]
        return [remote(own, own, base[name] + k, base[name] + k, z_peer(k)) for k in Z_ORDER]

    def a2_copies(pln, name, x_ref):
        return [
            remote(x_ref.at[0, pln.block(0)], x_ref.at[0, pln.block(k)], base[name] + k, base[name] + k, pln.peer2(k))
            for k in pln.order2
        ]

    def a2_factor_copies(pln, name, fac):
        part = fac.at[c, y]
        return [remote(part, part, base[name] + k, base[name] + k, y_peer(k)) for k in Y_ORDER]

    def forward(pln, name, x_ref, k):
        return remote(x_ref.at[0, pln.block(k)], x_ref.at[1, pln.block(k)], base[name] + k, base[name], sibling)

    def assemble(pln, s1, x_ref, chunks):
        parts = [s1[k].astype(F32) for k in range(pln.n1)]
        for j in range(chunks):
            tile = jnp.concatenate([part[OWN * j : OWN * (j + 1)] for part in parts], axis=0)
            x_ref[0, 0 : pln.rows, j * LANES : (j + 1) * LANES] = tile.astype(BF16)

    def per_core(fn):
        for pln in planes:
            pl.when(c == pln.core)(functools.partial(fn, pln))

    def hidden_copies(name, h_ref):
        copies = []
        for dx, dz in ((2, 1), (2, 0), (1, 0), (3, 1), (3, 0), (1, 1), (0, 1)):
            x = (t // 2 + dx) % 4
            b = x + 4 * ((t + dz + x) % 2)
            copies.append(remote(h_ref.at[pos], h_ref.at[pos], base[name] + b, base[name] + pos, (g, block_target(b))))
        return copies

    def wait_hidden(name, h_ref, blocks):
        for b in blocks:
            def wait(b=b):
                remote(h_ref.at[b], h_ref.at[b], base[name] + b, base[name] + b, (g, block_target(b))).wait_recv()
            pl.when(b != pos)(wait)

    def gather_first(pln):
        olds, news = a1_copies(pln, "a1o", s1_old), a1_copies(pln, "a1n", s1_new)
        lefts, rights = a1_factor_copies(pln, "a1l", left), a1_factor_copies(pln, "a1r", right)
        seconds = a2_copies(pln, "a2o", x_old)
        for copy in olds + hidden_copies("sq", square):
            copy.start()
        s1_new[0] = jnp.concatenate(scaled(new_v), axis=0).astype(BF16)
        for copy in news:
            copy.start()
        for load in small[3:]:
            load.wait()
        left[c, y, zh] = jnp.concatenate([gl_v[...], ul_v[...]], axis=1)
        for copy in olds:
            copy.wait_recv()
        assemble(pln, s1_old, x_old, CHUNKS)
        for copy in seconds:
            copy.start()
        forward(pln, "fo", x_old, 0).start()
        for copy in lefts:
            copy.start()
        wait_hidden("sq", square, range(NT))
        total = square[0]
        for b in range(1, NT):
            total += square[b]
        inverse = lax.rsqrt(total * (1.0 / D) + 1e-05)
        high = inverse.astype(BF16).astype(F32)
        low = inverse - high
        lane = lax.broadcasted_iota(jnp.int32, (8, LANES - R), 1)
        beside = jnp.zeros((8, LANES - R), F32)
        for n, column in enumerate((high[:, 0:1], low[:, 0:1], high[:, 1:2], low[:, 1:2])):
            beside = jnp.where(lane == n, column, beside)
        beside = jnp.concatenate([beside, jnp.zeros((8, LANES - R), F32)], axis=0)
        right[c, y, zh] = jnp.concatenate([dr_v[...].astype(F32), beside], axis=1).astype(BF16)
        for copy in rights:
            copy.start()
        for copy in news:
            copy.wait_recv()
        assemble(pln, s1_new, x_new, CHUNKS)
        for copy in seconds:
            copy.wait_send()
        for copy in a2_copies(pln, "a2n", x_new):
            copy.start()
        forward(pln, "fn", x_new, 0).start()

    per_core(gather_first)
    for load in loads:
        load.wait()

    def gather_second(pln, name, forward_name, x_ref):
        copies = a2_copies(pln, name, x_ref)
        for k, copy in reversed(list(zip(pln.order2, copies))):
            copy.wait_recv()
            forward(pln, forward_name, x_ref, k).start()

    def wait_sibling_half(name, x_ref):
        remote(x_ref.at[0], x_ref.at[1], base[name], base[name], sibling).wait_recv()

    def reduce_copy(name, p_ref, t_ref, b):
        return remote(p_ref.at[b], t_ref.at[pos], base[name] + b, base[name] + pos, (g, block_target(b)))

    def project(half, x_ref, p_ref, t_ref, name):
        product = lax.dot_general(
            x_ref[half, :, 0:DL], w_in[...], (((1,), (1,)), ((), ())), preferred_element_type=F32
        )
        p_ref[4 * half : 4 * half + 4, :, 0 : 2 * FL] = product.astype(BF16).reshape(4, BLOCK, 2 * FL)
        for b in range(4 * half, 4 * half + 4):
            pl.when(b != pos)(lambda b=b: reduce_copy(name, p_ref, t_ref, b).start())

    def reduced(p_ref, t_ref, name):
        t_ref[pos] = p_ref[pos]
        for b in range(NT):
            def wait(b=b):
                remote(p_ref.at[b], t_ref.at[b], base[name] + b, base[name] + b, (g, block_target(b))).wait_recv()
            pl.when(b != pos)(wait)
        total = t_ref[0].astype(F32)
        for b in range(1, NT):
            total += t_ref[b].astype(F32)
        return total

    def activate(gate, up, h_ref):
        h_ref[pos] = (gate / (1.0 + jnp.exp(-gate)) * up).astype(BF16)

    def spread(name, h_ref):
        for copy in hidden_copies(name, h_ref):
            copy.start()

    def c1_copies(pln, name, cs_ref, r1_ref):
        return [
            remote(cs_ref.at[pln.block(k)], r1_ref.at[pln.block(k)], base[name] + k, base[name] + k, pln.peer2(-k))
            for k in pln.order2
        ]

    def c2_copies(pln, name, c2_ref, r2_ref):
        return [
            remote(c2_ref.at[k], r2_ref.at[k], base[name] + k, base[name] + k, pln.peer1(-k)) for k in pln.order1
        ]

    def exchange_piece(name, d_sib, e_ref, piece):
        rows = pl.ds(piece * PIECE, PIECE)
        return remote(d_sib.at[rows], e_ref.at[rows], base[name] + piece, base[name] + piece, sibling)

    def down_project(h_name, h_ref, down_ref, d_sib, e_ref, e_name, cs_ref, c1_name, r1_ref):
        def product(half, piece):
            first = 4 * half + 2 * piece
            wait_hidden(h_name, h_ref, (first, first + 1))
            return jnp.dot(
                h_ref[first : first + 2].reshape(PIECE, FL), down_ref[...], preferred_element_type=F32
            )

        for piece in (1, 0):
            d_sib[piece * PIECE : (piece + 1) * PIECE] = product(1, piece).astype(BF16)
            exchange_piece(e_name, d_sib, e_ref, piece).start()
        for piece in (1, 0):
            rows = pl.ds(piece * PIECE, PIECE)
            own = product(0, piece)
            exchange_piece(e_name, d_sib, e_ref, piece).wait_recv()
            cs_ref[rows] = (own + e_ref[rows].astype(F32)).astype(BF16)

            def start(pln, piece=piece):
                n = PIECE // pln.rows
                for k, copy in zip(pln.order2, c1_copies(pln, c1_name, cs_ref, r1_ref)):
                    if k // n == piece:
                        copy.start()

            per_core(start)

    def scatter_second(pln, name1, cs_ref, r1_ref, name2, c2_ref, r2_ref):
        for copy in c1_copies(pln, name1, cs_ref, r1_ref):
            copy.wait_recv()
        total = cs_ref[pln.block(0)].astype(F32)
        for k in range(1, pln.n2):
            total += r1_ref[pln.block(k)].astype(F32)
        def put(k):
            piece = jnp.concatenate(fold(total[OWN * k : OWN * (k + 1)]), axis=0)
            c2_ref[k] = piece.astype(BF16)

        for k, copy in zip(pln.order1, c2_copies(pln, name2, c2_ref, r2_ref)):
            put(k)
            copy.start()
        put(0)

    def scatter_last(pln, name2, c2_ref, r2_ref, out_ref):
        for copy in c2_copies(pln, name2, c2_ref, r2_ref):
            copy.wait_recv()
        total = c2_ref[0].astype(F32)
        for k in range(1, pln.n1):
            total += r2_ref[k].astype(F32)
        out_ref[...] = jnp.concatenate(
            [total[OWN * j : OWN * (j + 1)] for j in range(CHUNKS)], axis=1
        ).astype(BF16)

    per_core(lambda pln: gather_second(pln, "a2o", "fo", x_old))
    project(0, x_old, p_old, t_old, "to")
    wait_sibling_half("fo", x_old)
    project(1, x_old, p_old, t_old, "to")

    def gather_rest(pln):
        gather_second(pln, "a2n", "fn", x_new)
        for copy in a2_copies(pln, "a2n", x_new):
            copy.wait_send()
        for name1, name2, fac in (("a1l", "a2l", left), ("a1r", "a2r", right)):
            for copy in a1_factor_copies(pln, name1, fac):
                copy.wait_recv()
            for copy in a2_factor_copies(pln, name2, fac):
                copy.start()

    per_core(gather_rest)
    for b in range(NT):
        pl.when(b != pos)(lambda b=b: reduce_copy("to", p_old, t_old, b).wait_send())
    project(0, x_new, p_new, t_new, "tn")
    wait_sibling_half("fn", x_new)
    project(1, x_new, p_new, t_new, "tn")

    def exchange_factors(name2, name, fac):
        def wait(pln):
            for copy in a2_factor_copies(pln, name2, fac):
                copy.wait_recv()

        per_core(wait)
        copy = remote(fac.at[c], fac.at[c], base[name], base[name], sibling)
        copy.start()
        return copy

    left_exchange = exchange_factors("a2l", "fl", left)
    left_exchange.wait_recv()
    low = jnp.zeros((ROWS, 2 * R), F32)
    for q in range(NZ):
        part = jnp.concatenate([left[i % 2, i // 2, q] for i in range(2 * NY)], axis=0)
        columns = x_new[:, :, q * 256 : (q + 1) * 256].reshape(ROWS, 256)
        low += jnp.dot(columns, part, preferred_element_type=F32)
    p_low[...] = low.astype(BF16).reshape(NT, BLOCK, 2 * R)
    for b in range(NT):
        pl.when(b != pos)(lambda b=b: reduce_copy("tl", p_low, t_low, b).start())
    right_exchange = exchange_factors("a2r", "fr", right)

    total = reduced(p_old, t_old, "to")
    right_exchange.wait_recv()
    core, i = c + (1 - 2 * c) * (pos // 4), pos % 4
    rows = []
    for n in range(8):
        ky = (1 - core) * (2 * i + n // 4) + core * n
        kz = (1 - core) * (n % 4) + core * i
        rows.append(right[core, (y - ky + NY) % NY, (zh - kz + NZ) % NZ].astype(F32)[0:OWN])
    inverse = jnp.concatenate(rows, axis=0)
    inverse_old = inverse[:, R : R + 1] + inverse[:, R + 1 : R + 2]
    inverse_new = inverse[:, R + 2 : R + 3] + inverse[:, R + 3 : R + 4]
    activate(total[:, 0:FL] * inverse_old, total[:, FL : 2 * FL] * inverse_old, h_old)

    for b in range(NT):
        pl.when(b != pos)(lambda b=b: reduce_copy("tn", p_new, t_new, b).wait_send())
    spread("ho", h_old)

    total = reduced(p_new, t_new, "tn")
    low = reduced(p_low, t_low, "tl").astype(BF16)
    gate = total[:, 0:FL] + ALPHA / R * jnp.dot(low[:, 0:R], gr_v[...], preferred_element_type=F32)
    up = total[:, FL : 2 * FL] + ALPHA / R * jnp.dot(low[:, R : 2 * R], ur_v[...], preferred_element_type=F32)
    activate(gate * inverse_new, up * inverse_new, h_new)
    spread("hn", h_new)
    for q in range(NZ):
        columns = pl.ds(q * 256, 256)
        part = jnp.concatenate([right[i % 2, i // 2, q, :, 0:R] for i in range(2 * NY)], axis=0)
        product = lax.dot_general(dl_v[...], part, (((0,), (1,)), ((), ())), preferred_element_type=F32)
        down_new[:, columns] = (down_v[:, columns].astype(F32) + ALPHA / R * product).astype(BF16)

    down_project("ho", h_old, down_v, d_sib_old, e_old, "eo", cs_old, "c1o", r1_old)

    down_project("hn", h_new, down_new, d_sib_new, e_new, "en", cs_new, "c1n", r1_new)
    per_core(lambda pln: scatter_second(pln, "c1o", cs_old, r1_old, "c2o", c2_old, r2_old))
    per_core(lambda pln: scatter_second(pln, "c1n", cs_new, r1_new, "c2n", c2_new, r2_new))
    per_core(lambda pln: scatter_last(pln, "c2o", c2_old, r2_old, out_old_ref))

    def drain(pln):
        copies = a1_copies(pln, "a1o", s1_old) + a1_copies(pln, "a1n", s1_new)
        copies += a1_factor_copies(pln, "a1l", left) + a1_factor_copies(pln, "a1r", right)
        copies += a2_factor_copies(pln, "a2l", left) + a2_factor_copies(pln, "a2r", right)
        copies += [forward(pln, "fo", x_old, k) for k in range(pln.n2)]
        copies += [forward(pln, "fn", x_new, k) for k in range(pln.n2)]
        copies += c1_copies(pln, "c1o", cs_old, r1_old) + c1_copies(pln, "c1n", cs_new, r1_new)
        copies += c2_copies(pln, "c2o", c2_old, r2_old) + c2_copies(pln, "c2n", c2_new, r2_new)
        for copy in copies:
            copy.wait_send()

    per_core(drain)
    left_exchange.wait_send()
    right_exchange.wait_send()
    for piece in (1, 0):
        exchange_piece("eo", d_sib_old, e_old, piece).wait_send()
        exchange_piece("en", d_sib_new, e_new, piece).wait_send()
    for b in range(NT):
        def wait(b=b):
            reduce_copy("tl", p_low, t_low, b).wait_send()
        pl.when(b != pos)(wait)
    for copy in hidden_copies("sq", square) + hidden_copies("ho", h_old) + hidden_copies("hn", h_new):
        copy.wait_send()

    per_core(lambda pln: scatter_last(pln, "c2n", c2_new, r2_new, out_new_ref))


def hand_over(old_ref, new_ref, out_old_ref, out_new_ref, sem):
    copies = [
        pltpu.make_async_copy(old_ref, out_old_ref, sem.at[0]),
        pltpu.make_async_copy(new_ref, out_new_ref, sem.at[1]),
    ]
    for copy in copies:
        copy.start()
    for copy in copies:
        copy.wait()


def per_device(old, new, gain, gate, up, down, gl, gr, ul, ur, dl, dr):
    vmem = pl.BlockSpec(memory_space=pltpu.VMEM)
    hbm = pl.BlockSpec(memory_space=pl.ANY)
    scratch = [
        ((OWN, DL), BF16), ((OWN, DL), BF16), ((1, DL), F32),
        ((16, R), BF16), ((16, R), BF16), ((16, R), BF16),
        ((R, FL), BF16), ((R, FL), BF16), ((R, FL), BF16),
        ((2 * FL, DL), BF16), ((FL, DL), BF16), ((FL, DL), BF16),
        ((8, 32, LANES), BF16), ((8, 32, LANES), BF16),
        ((2, NY, NZ, 16, LANES), BF16), ((2, NY, NZ, 16, LANES), BF16),
        ((2, HALF, DL), BF16), ((2, HALF, DL), BF16),
        ((NT, BLOCK, 2 * FL), BF16), ((NT, BLOCK, 2 * FL), BF16), ((NT, BLOCK, 2 * R), BF16),
        ((NT, BLOCK, 2 * FL), BF16), ((NT, BLOCK, 2 * FL), BF16), ((NT, BLOCK, 2 * R), BF16),
        ((NT, BLOCK, FL), BF16), ((NT, BLOCK, FL), BF16),
        ((HALF, DL), BF16), ((HALF, DL), BF16),
        ((HALF, DL), BF16), ((HALF, DL), BF16), ((HALF, DL), BF16), ((HALF, DL), BF16),
        ((HALF, DL), BF16), ((HALF, DL), BF16),
        ((8, 32, LANES), BF16), ((8, 32, LANES), BF16), ((8, 32, LANES), BF16), ((8, 32, LANES), BF16),
        ((NT, 8, LANES), F32),
    ]
    flops = 2 * (2 * ROWS * DL * FL * 3 + 3 * DL * FL * R)
    out_shape = [jax.ShapeDtypeStruct((OWN, DL), BF16)] * 2
    outs = pl.pallas_call(
        kernel,
        out_shape=out_shape,
        in_specs=[hbm] * 12,
        out_specs=[vmem, vmem],
        scratch_shapes=[pltpu.VMEM(shape, dtype) for shape, dtype in scratch]
        + [pltpu.SemaphoreType.DMA((12,)), pltpu.SemaphoreType.DMA((168,)), pltpu.SemaphoreType.DMA((168,))],
        compiler_params=pltpu.CompilerParams(
            collective_id=0, has_side_effects=True, vmem_limit_bytes=60 * 1024 * 1024
        ),
        cost_estimate=pl.CostEstimate(flops=flops, bytes_accessed=6 * DL * FL, transcendentals=2 * BLOCK * FL),
    )(old, new, gain.reshape(1, DL), gl, ul, dr, gr, ur, dl.T, gate.T, up.T, down)
    return pl.pallas_call(
        hand_over,
        out_shape=out_shape,
        in_specs=[vmem, vmem],
        out_specs=[hbm, hbm],
        scratch_shapes=[pltpu.SemaphoreType.DMA((2,))],
    )(*outs)


def solution(mesh):
    in_specs = (
        P("groups", "tensor"),
        P("groups", "tensor"),
        P("tensor"),
        P("tensor", "groups"),
        P("tensor", "groups"),
        P("groups", "tensor"),
        P(("tensor", "groups"), None),
        P(None, "groups"),
        P(("tensor", "groups"), None),
        P(None, "groups"),
        P("groups", None),
        P(("tensor", "groups"), None),
    )
    out_specs = (P("groups", "tensor"), P("groups", "tensor"))
    return jax.shard_map(per_device, mesh=mesh, in_specs=in_specs, out_specs=out_specs, check_vma=False)
```
